256 devices in a mesh: row: 8 (over y, core), col: 32 (over z, x).
Axes of the slice: x: 4, y: 4, z: 8, core: 2. Of those that a mesh axis runs over, the one named last changes fastest.
Arguments:
- matrix: float32 [16384, 16384], P('row', 'col'), as said below
Outputs:
- updated: float32 [16384, 16384], P('row', 'col')
- reflectors: float32 [1, 16384, 256], P(None, ('row', 'col'))
- products: float32 [1, 16384, 256], P(None, ('row', 'col'))
Inputs may be any that keep to these rules, and one draw needn't show every extreme that they name: `matrix`: symmetric.
All inputs are finite; a program needn't handle non-finite values.
Results may differ from the reference program's by a relative error of at most 0.0003.
Values sent between devices are 32-bit elements; how exact they have to be, the bound alone decides.
No kernel may reach another device: no remote copies, remote signals or barrier semaphores. Data moves between devices by JAX's collectives and lax.ppermute only.
A program may use at most 64 MiB of HBM per device.

```python
import math
import jax
import jax.numpy as jnp
from jax import lax

ORDER = 16384
NB = 256
PANELS = 1


def draw_matrix(key, part):
    noise_key = jax.random.fold_in(key, 11)
    block_key = jax.random.fold_in(key, 23)
    noise = jax.random.normal(noise_key, (ORDER, ORDER), jnp.float32)
    sym_part = (noise + noise.T) * 0.7071
    diag_scale = 2.0 * math.sqrt(ORDER)
    spread = 0.35 * diag_scale / math.sqrt(NB)
    blocks = jax.random.normal(block_key, (2, NB, NB), jnp.float32) * spread
    blocks = blocks + diag_scale * jnp.eye(NB, dtype=jnp.float32)[None, :, :]
    planted = jnp.zeros((ORDER, ORDER), jnp.float32)
    planted = planted.at[NB:2 * NB, 0:NB].set(blocks[0])
    planted = planted.at[2 * NB:3 * NB, NB:2 * NB].set(blocks[1])
    result = sym_part + planted + planted.T
    return result


def setup_inputs(seed: int = 0) -> dict:
    key_of = jax.random.split(jax.random.key(seed), 2)
    matrix = draw_matrix(jax.random.fold_in(key_of[1], 71), 0)
    return {"matrix": matrix}


def matmul(left, right):
    return jnp.dot(left.astype(jnp.float32), right.astype(jnp.float32), precision=lax.Precision.HIGHEST, preferred_element_type=jnp.float32)

def lu_signed(square):
    order_n = square.shape[0]
    all_ids = jnp.arange(order_n)

    def lu_step(pivot_idx, state):
        work_mat, sign_vec = state
        column = work_mat[:, pivot_idx]
        raw_pivot = column[pivot_idx]
        sign_now = jnp.where(raw_pivot >= 0, 1.0, -1.0)
        pivot_val = raw_pivot + sign_now
        lower_col = jnp.where(all_ids > pivot_idx, column / pivot_val, 0.0)
        upper_row = jnp.where(all_ids > pivot_idx, work_mat[pivot_idx, :], 0.0)
        work_mat = work_mat - lower_col[:, None] * upper_row[None, :]
        kept = jnp.where(all_ids > pivot_idx, lower_col, jnp.where(all_ids == pivot_idx, pivot_val, column))
        work_mat = work_mat.at[:, pivot_idx].set(kept)
        sign_vec = sign_vec.at[pivot_idx].set(sign_now)
        return (work_mat, sign_vec)
    packed, sign_vec = lax.fori_loop(0, order_n, lu_step, (square, jnp.zeros((order_n,), square.dtype)))
    unit_lower = jnp.tril(packed, -1) + jnp.eye(order_n, dtype=square.dtype)
    return (unit_lower, jnp.triu(packed), sign_vec)

def reference(matrix):
    row_ids = jnp.arange(matrix.shape[0])
    current = matrix
    all_refl = []
    all_prod = []
    for panel_idx in range(PANELS):
        col_start = panel_idx * NB
        row_start = col_start + NB
        panel_cols = jnp.where((row_ids >= row_start)[:, None], current[:, col_start:col_start + NB], 0.0)
        gram_sum = matmul(panel_cols.T, panel_cols)
        chol_low = jnp.linalg.cholesky(gram_sum)
        q_basis = jax.scipy.linalg.solve_triangular(chol_low, panel_cols.T, lower=True).T
        top_block = q_basis[row_start:row_start + NB]
        unit_lower, upper_tri, sign_diag = lu_signed(top_block)
        solved = jax.scipy.linalg.solve_triangular(upper_tri.T, q_basis.T, lower=True).T
        rel_pos = row_ids - row_start
        in_top = (rel_pos >= 0) & (rel_pos < NB)
        lower_rows = jnp.take(unit_lower, jnp.clip(rel_pos, 0, NB - 1), axis=0)
        refl = jnp.where(in_top[:, None], lower_rows, jnp.where((rel_pos < 0)[:, None], 0.0, solved))
        scaled = upper_tri * sign_diag[None, :]
        t_factor = jax.scipy.linalg.solve_triangular(unit_lower, scaled.T, lower=True, unit_diagonal=True).T
        x_rows = matmul(current, matmul(refl, t_factor))
        inner_prod = matmul(refl.T, x_rows)
        w_rows = x_rows - 0.5 * matmul(refl, matmul(t_factor.T, inner_prod))
        current = current - matmul(refl, w_rows.T) - matmul(w_rows, refl.T)
        all_refl.append(refl)
        all_prod.append(w_rows)
    return (current, jnp.stack(all_refl), jnp.stack(all_prod))
```

```python
import jax
import jax.numpy as jnp
from jax import lax
from jax.experimental import pallas as pl
from jax.experimental.pallas import tpu as pltpu
from jax.sharding import PartitionSpec as P

HI = lax.Precision.HIGHEST
NB = 256
BK = 64
STEPS = NB // BK
LOOK = 8


def dot(a, b, ca=1, cb=0):
    return lax.dot_general(a, b, (((ca,), (cb,)), ((), ())), precision=HI, preferred_element_type=jnp.float32)


def lanes_of(chunk, k):
    return jnp.broadcast_to(chunk[:, k : k + 1], chunk.shape)


def leaf_start(block, below):
    eye = jnp.eye(BK, dtype=jnp.float32)
    top = jnp.concatenate([block, eye], axis=1)
    rows = [top[8 * i : 8 * i + 8] for i in range(BK // 8)]
    if below:
        low = jnp.concatenate([eye, jnp.zeros((BK, BK), jnp.float32)], axis=1)
        rows += [low[8 * i : 8 * i + 8] for i in range(BK // 8)]
    return {"rows": rows, "below": below, "recip": [], "sign": [], "pivot": []}


def leaf_group(state, first, look, signed):
    rows = state["rows"]
    half = BK // 8
    lane = lax.broadcasted_iota(jnp.int32, (1, 2 * BK), 1)
    sub = lax.broadcasted_iota(jnp.int32, (8, 2 * BK), 0)
    active = list(range(first // 8, half))
    if state["below"]:
        active += list(range(half, half + (first + look - 1) // 8 + 1))
    cols = [{i: lanes_of(rows[i], first + j) for i in active} for j in range(look)]
    for j in range(look):
        k = first + j
        own, off = k // 8, k % 8
        pivot = cols[j][own][off : off + 1]
        if signed:
            sign = jnp.where(pivot >= 0, 1.0, -1.0).astype(jnp.float32)
            pivot = pivot + sign
            state["sign"].append(sign)
        recip = 1.0 / pivot
        state["recip"].append(recip)
        state["pivot"].append(pivot)
        scaled = jnp.where(lane > k, rows[own][off : off + 1] * recip, 0.0)
        ahead = [cols[jj][own][off : off + 1] * recip for jj in range(j + 1, look)]
        for i in active:
            if i < half and i == own:
                if off == 7:
                    continue
                mult = jnp.where(sub > off, cols[j][i], 0.0)
            else:
                mult = cols[j][i]
            rows[i] = rows[i] - mult * scaled
            for n, jj in enumerate(range(j + 1, look)):
                cols[jj][i] = cols[jj][i] - mult * ahead[n]


def pick(rows):
    lane = lax.broadcasted_iota(jnp.int32, (1, 2 * BK), 1)
    out = jnp.zeros((1, 2 * BK), jnp.float32)
    for k, row in enumerate(rows):
        out = jnp.where(lane == k, row, out)
    return out[:, :BK]


def factor_step(p, refs):
    h_ref, l_ref, u_ref, li_ref, ui_ref, s_ref, y_ref = refs
    chol = lu = None
    if p < STEPS:
        chol = leaf_start(h_ref[p * BK : (p + 1) * BK, p * BK : (p + 1) * BK], False)
    if p > 0:
        lu = leaf_start(y_ref[(p - 1) * BK : p * BK, :], True)
    for first in range(0, BK, LOOK):
        if chol is not None:
            leaf_group(chol, first, LOOK, False)
        if lu is not None:
            leaf_group(lu, first, LOOK, True)
    tri_r = lax.broadcasted_iota(jnp.int32, (BK, BK), 0)
    tri_c = lax.broadcasted_iota(jnp.int32, (BK, BK), 1)
    half = BK // 8
    if chol is not None:
        inv_low = jnp.concatenate(chol["rows"], axis=0)[:, BK:]
        recip = pick(chol["recip"])
        scale = jnp.sqrt(recip)
        panel = dot(h_ref[:, p * BK : (p + 1) * BK], inv_low, 1, 1) * scale
        h_ref[:, p * BK : (p + 1) * BK] = panel
        if p + 1 < STEPS:
            after = panel[(p + 1) * BK : NB]
            h_ref[:, (p + 1) * BK :] = h_ref[:, (p + 1) * BK :] - dot(panel, after, 1, 1)
    if lu is not None:
        q0, q1 = (p - 1) * BK, p * BK
        full = jnp.concatenate(lu["rows"][:half], axis=0)
        low_inv = full[:, BK:]
        recip = pick(lu["recip"])
        pivot = pick(lu["pivot"])
        s_ref[:, q0:q1] = pick(lu["sign"])
        main = full[:, :BK]
        l_diag = jnp.where(tri_r > tri_c, main * recip, jnp.where(tri_r == tri_c, 1.0, 0.0))
        u_diag = jnp.where(tri_r < tri_c, main, jnp.where(tri_r == tri_c, pivot, 0.0))
        low = jnp.concatenate(lu["rows"][half:], axis=0)[:, :BK]
        u_inv = jnp.where(tri_r <= tri_c, low * recip, 0.0)
        l_ref[q0:q1, q0:q1] = l_diag
        u_ref[q0:q1, q0:q1] = u_diag
        li_ref[q0:q1, q0:q1] = low_inv
        ui_ref[q0:q1, q0:q1] = u_inv
        if p < STEPS:
            l_ref[q1:, q0:q1] = dot(y_ref[q1:, :], u_inv)
        if p > 1:
            li_ref[q0:q1, :q0] = -dot(low_inv, dot(l_ref[q0:q1, :q0], li_ref[:q0, :q0]))
            ui_ref[:q0, q0:q1] = -dot(ui_ref[:q0, :q0], dot(u_ref[:q0, q0:q1], u_inv))
    if p < STEPS:
        q1 = p * BK
        col = h_ref[NB : 2 * NB, p * BK : (p + 1) * BK]
        if p > 0:
            upper = dot(li_ref[:q1, :q1], col[:q1])
            u_ref[:q1, q1 : q1 + BK] = upper
            y_ref[q1:, :] = col[q1:] - dot(l_ref[q1:, :q1], upper)
        else:
            y_ref[...] = col


def factor_all(gram, top):
    def kernel(g_ref, c_ref, l_out, u_out, li_out, m_out, ri_out, s_out, h, y, ui):
        h[:NB] = g_ref[...]
        h[NB : 2 * NB] = c_ref[...]
        r = lax.broadcasted_iota(jnp.int32, (NB, NB), 0)
        c = lax.broadcasted_iota(jnp.int32, (NB, NB), 1)
        h[2 * NB :] = jnp.where(r == c, 1.0, 0.0).astype(jnp.float32)
        for ref in (l_out, u_out, li_out, ui):
            ref[...] = jnp.zeros((NB, NB), jnp.float32)
        for p in range(STEPS + 1):
            factor_step(p, (h, l_out, u_out, li_out, ui, s_out, y))
        r_inv = h[2 * NB :]
        m_out[...] = dot(r_inv, ui[...])
        ri_out[...] = r_inv * s_out[...]

    sq = jax.ShapeDtypeStruct((NB, NB), jnp.float32)
    return pl.pallas_call(
        kernel,
        out_shape=[sq, sq, sq, sq, sq, jax.ShapeDtypeStruct((1, NB), jnp.float32)],
        scratch_shapes=[
            pltpu.VMEM((3 * NB, NB), jnp.float32),
            pltpu.VMEM((NB, BK), jnp.float32),
            pltpu.VMEM((NB, NB), jnp.float32),
        ],
        compiler_params=pltpu.CompilerParams(vmem_limit_bytes=24 * 1024 * 1024),
        cost_estimate=pl.CostEstimate(flops=20_000_000_000, bytes_accessed=2_000_000, transcendentals=0),
        name="factor",
    )(gram, top)


def mm(left, right, ca=1, cb=0, precision=lax.Precision.HIGH):
    return lax.dot_general(
        left, right, (((ca,), (cb,)), ((), ())), precision=precision, preferred_element_type=jnp.float32
    )


XS, ZS, RS = 4, 8, 8
X_GROUPS = [[z * XS + x for x in range(XS)] for z in range(ZS)]
Z_GROUPS = [[z * XS + x for z in range(ZS)] for x in range(XS)]


def exchange(value, axis, groups=None):
    return lax.all_to_all(value, axis, 0, 0, tiled=True, axis_index_groups=groups)


def to_all(value, count, axis, groups=None):
    return exchange(jnp.broadcast_to(value[None], (count, *value.shape)), axis, groups)


def x_shift(value, k):
    pairs = [(z * XS + x, z * XS + (x + k) % XS) for z in range(ZS) for x in range(XS)]
    return lax.ppermute(value, "col", pairs)


def swap(value):
    cols = ZS * XS
    pairs = [
        (r * cols + z * XS + x, z * cols + r * XS + x)
        for r in range(RS)
        for z in range(ZS)
        for x in range(XS)
    ]
    return lax.ppermute(value, ("row", "col"), pairs)


def gather_x(value, x_index):
    rows = value.shape[0]
    out = jnp.zeros((XS * rows, value.shape[1]), value.dtype)
    out = lax.dynamic_update_slice_in_dim(out, value, x_index * rows, 0)
    for k in (1, 3, 2):
        got = x_shift(value, k)
        out = lax.dynamic_update_slice_in_dim(out, got, (x_index + XS - k) % XS * rows, 0)
    return out


def body(matrix):
    rows, cols = matrix.shape
    row_index = lax.axis_index("row")
    col_index = lax.axis_index("col")
    z_index, x_index = col_index // XS, col_index % XS
    piece = cols // RS

    row_ids = row_index * rows + jnp.arange(rows)
    own_strip = jnp.where((row_ids >= NB)[:, None], matrix[:, :NB], 0.0)
    gram = mm(own_strip, own_strip, 0, 0, HI)
    top = matrix[NB : 2 * NB, :NB]
    turned = matrix[: 2 * NB, :].T
    col_ids = col_index * cols + jnp.arange(cols)
    strip_turned = jnp.where((col_ids >= NB)[:, None], turned[:, :NB], 0.0)
    next_turned = turned[:, NB:]
    share = NB // RS
    sent = jnp.concatenate(
        [
            gram.reshape(RS, share, NB),
            top.reshape(RS, share, NB),
            strip_turned.reshape(RS, piece, NB),
            next_turned.reshape(RS, piece, NB),
        ],
        axis=1,
    )
    got = exchange(sent, "row")
    gram_share = jnp.sum(got[:, :share], axis=0)
    small = jnp.concatenate([gram_share, got[0, share : 2 * share]], axis=0)
    strip_piece = got[0, 2 * share : 2 * share + piece]
    next_piece = swap(got[0, 2 * share + piece :])

    strip_cols = to_all(strip_piece, RS, "row").reshape(cols, NB)
    partial = mm(matrix, strip_cols)
    quarter = rows // XS
    prod = lax.dynamic_slice_in_dim(partial, x_index * quarter, quarter, 0)
    for k in (1, 3, 2):
        prod = prod + x_shift(
            lax.dynamic_slice_in_dim(partial, (x_index + k) % XS * quarter, quarter, 0), k
        )
    prod = jnp.sum(exchange(prod.reshape(ZS, piece, NB), "col", Z_GROUPS), axis=0)
    strip_rows = gather_x(swap(strip_cols), x_index)

    small = to_all(small, XS, "col", X_GROUPS)[0]
    small = to_all(small, ZS, "col", Z_GROUPS)[0]
    small = to_all(small, RS, "row")
    gram_sum = small[:, :share].reshape(NB, NB)
    top_block = small[:, share:].reshape(NB, NB)
    low, up, low_inv, to_v, to_x, sign = factor_all(gram_sum, top_block)

    x_piece = mm(mm(prod, to_x, 1, 0, HI) + next_piece, low_inv, 1, 1, HI)
    x_some = to_all(x_piece, ZS, "col", Z_GROUPS).reshape(cols, NB)
    x_cols = swap(x_some)
    x_rows = gather_x(x_some, x_index)

    def reflectors(strip, holds_top):
        out = mm(strip, to_v)
        return out.at[NB : 2 * NB].set(jnp.where(holds_top, low, out[NB : 2 * NB]))

    v_rows = reflectors(strip_rows, row_index == 0)
    v_cols = reflectors(strip_cols, col_index == 0)
    inner = mm(v_rows, x_rows, 0, 0)
    inner = jnp.sum(exchange(inner.reshape(RS, share, NB), "row"), axis=0)
    inner = to_all(inner, RS, "row").reshape(NB, NB)
    t_factor = mm(up * sign, low_inv, 1, 1, HI)
    half = 0.5 * mm(t_factor, inner, 0, 0, HI)
    w_rows = x_rows - mm(v_rows, half)
    w_cols = x_cols - mm(v_cols, half)
    left = jnp.concatenate([v_rows, w_rows], axis=1)
    right = jnp.concatenate([w_cols, v_cols], axis=1)
    updated = matrix - mm(left, right, 1, 1)
    out_rows = rows // (XS * ZS)
    v_out = lax.dynamic_slice_in_dim(v_rows, col_index * out_rows, out_rows, 0)
    w_out = lax.dynamic_slice_in_dim(w_rows, col_index * out_rows, out_rows, 0)
    return (updated, v_out[None], w_out[None])


def solution(mesh):
    return jax.shard_map(
        body,
        mesh=mesh,
        in_specs=(P("row", "col"),),
        out_specs=(P("row", "col"), P(None, ("row", "col"), None), P(None, ("row", "col"), None)),
        check_vma=False,
    )
```

```python
import jax
import jax.numpy as jnp
from jax import lax
from jax.experimental import pallas as pl
from jax.experimental.pallas import tpu as pltpu
from jax.sharding import PartitionSpec as P

HI = lax.Precision.HIGHEST
NB = 256
BK = 64
STEPS = NB // BK
LOOK = 8


def dot(a, b, ca=1, cb=0):
    return lax.dot_general(a, b, (((ca,), (cb,)), ((), ())), precision=HI, preferred_element_type=jnp.float32)


def lanes_of(chunk, k):
    return jnp.broadcast_to(chunk[:, k : k + 1], chunk.shape)


def leaf_start(block, below):
    eye = jnp.eye(BK, dtype=jnp.float32)
    top = jnp.concatenate([block, eye], axis=1)
    rows = [top[8 * i : 8 * i + 8] for i in range(BK // 8)]
    if below:
        low = jnp.concatenate([eye, jnp.zeros((BK, BK), jnp.float32)], axis=1)
        rows += [low[8 * i : 8 * i + 8] for i in range(BK // 8)]
    return {"rows": rows, "below": below, "recip": [], "sign": [], "pivot": []}


def leaf_group(state, first, look, signed):
    rows = state["rows"]
    half = BK // 8
    lane = lax.broadcasted_iota(jnp.int32, (1, 2 * BK), 1)
    sub = lax.broadcasted_iota(jnp.int32, (8, 2 * BK), 0)
    active = list(range(first // 8, half))
    if state["below"]:
        active += list(range(half, half + (first + look - 1) // 8 + 1))
    cols = [{i: lanes_of(rows[i], first + j) for i in active} for j in range(look)]
    for j in range(look):
        k = first + j
        own, off = k // 8, k % 8
        pivot = cols[j][own][off : off + 1]
        if signed:
            sign = jnp.where(pivot >= 0, 1.0, -1.0).astype(jnp.float32)
            pivot = pivot + sign
            state["sign"].append(sign)
        recip = 1.0 / pivot
        state["recip"].append(recip)
        state["pivot"].append(pivot)
        scaled = jnp.where(lane > k, rows[own][off : off + 1] * recip, 0.0)
        ahead = [cols[jj][own][off : off + 1] * recip for jj in range(j + 1, look)]
        for i in active:
            if i < half and i == own:
                if off == 7:
                    continue
                mult = jnp.where(sub > off, cols[j][i], 0.0)
            else:
                mult = cols[j][i]
            rows[i] = rows[i] - mult * scaled
            for n, jj in enumerate(range(j + 1, look)):
                cols[jj][i] = cols[jj][i] - mult * ahead[n]


def pick(rows):
    lane = lax.broadcasted_iota(jnp.int32, (1, 2 * BK), 1)
    out = jnp.zeros((1, 2 * BK), jnp.float32)
    for k, row in enumerate(rows):
        out = jnp.where(lane == k, row, out)
    return out[:, :BK]


def factor_step(p, refs):
    h_ref, l_ref, u_ref, li_ref, ui_ref, s_ref, y_ref = refs
    chol = lu = None
    if p < STEPS:
        chol = leaf_start(h_ref[p * BK : (p + 1) * BK, p * BK : (p + 1) * BK], False)
    if p > 0:
        lu = leaf_start(y_ref[(p - 1) * BK : p * BK, :], True)
    for first in range(0, BK, LOOK):
        if chol is not None:
            leaf_group(chol, first, LOOK, False)
        if lu is not None:
            leaf_group(lu, first, LOOK, True)
    tri_r = lax.broadcasted_iota(jnp.int32, (BK, BK), 0)
    tri_c = lax.broadcasted_iota(jnp.int32, (BK, BK), 1)
    half = BK // 8
    if chol is not None:
        inv_low = jnp.concatenate(chol["rows"], axis=0)[:, BK:]
        recip = pick(chol["recip"])
        scale = jnp.sqrt(recip)
        panel = dot(h_ref[:, p * BK : (p + 1) * BK], inv_low, 1, 1) * scale
        h_ref[:, p * BK : (p + 1) * BK] = panel
        if p + 1 < STEPS:
            after = panel[(p + 1) * BK : NB]
            h_ref[:, (p + 1) * BK :] = h_ref[:, (p + 1) * BK :] - dot(panel, after, 1, 1)
    if lu is not None:
        q0, q1 = (p - 1) * BK, p * BK
        full = jnp.concatenate(lu["rows"][:half], axis=0)
        low_inv = full[:, BK:]
        recip = pick(lu["recip"])
        pivot = pick(lu["pivot"])
        s_ref[:, q0:q1] = pick(lu["sign"])
        main = full[:, :BK]
        l_diag = jnp.where(tri_r > tri_c, main * recip, jnp.where(tri_r == tri_c, 1.0, 0.0))
        u_diag = jnp.where(tri_r < tri_c, main, jnp.where(tri_r == tri_c, pivot, 0.0))
        low = jnp.concatenate(lu["rows"][half:], axis=0)[:, :BK]
        u_inv = jnp.where(tri_r <= tri_c, low * recip, 0.0)
        l_ref[q0:q1, q0:q1] = l_diag
        u_ref[q0:q1, q0:q1] = u_diag
        li_ref[q0:q1, q0:q1] = low_inv
        ui_ref[q0:q1, q0:q1] = u_inv
        if p < STEPS:
            l_ref[q1:, q0:q1] = dot(y_ref[q1:, :], u_inv)
        if p > 1:
            li_ref[q0:q1, :q0] = -dot(low_inv, dot(l_ref[q0:q1, :q0], li_ref[:q0, :q0]))
            ui_ref[:q0, q0:q1] = -dot(ui_ref[:q0, :q0], dot(u_ref[:q0, q0:q1], u_inv))
    if p < STEPS:
        q1 = p * BK
        col = h_ref[NB : 2 * NB, p * BK : (p + 1) * BK]
        if p > 0:
            upper = dot(li_ref[:q1, :q1], col[:q1])
            u_ref[:q1, q1 : q1 + BK] = upper
            y_ref[q1:, :] = col[q1:] - dot(l_ref[q1:, :q1], upper)
        else:
            y_ref[...] = col


def factor_all(gram, top):
    def kernel(g_ref, c_ref, l_out, u_out, li_out, m_out, ri_out, s_out, h, y, ui):
        h[:NB] = g_ref[...]
        h[NB : 2 * NB] = c_ref[...]
        r = lax.broadcasted_iota(jnp.int32, (NB, NB), 0)
        c = lax.broadcasted_iota(jnp.int32, (NB, NB), 1)
        h[2 * NB :] = jnp.where(r == c, 1.0, 0.0).astype(jnp.float32)
        for ref in (l_out, u_out, li_out, ui):
            ref[...] = jnp.zeros((NB, NB), jnp.float32)
        for p in range(STEPS + 1):
            factor_step(p, (h, l_out, u_out, li_out, ui, s_out, y))
        r_inv = h[2 * NB :]
        m_out[...] = dot(r_inv, ui[...])
        ri_out[...] = r_inv * s_out[...]

    sq = jax.ShapeDtypeStruct((NB, NB), jnp.float32)
    return pl.pallas_call(
        kernel,
        out_shape=[sq, sq, sq, sq, sq, jax.ShapeDtypeStruct((1, NB), jnp.float32)],
        scratch_shapes=[
            pltpu.VMEM((3 * NB, NB), jnp.float32),
            pltpu.VMEM((NB, BK), jnp.float32),
            pltpu.VMEM((NB, NB), jnp.float32),
        ],
        compiler_params=pltpu.CompilerParams(vmem_limit_bytes=24 * 1024 * 1024),
        cost_estimate=pl.CostEstimate(flops=20_000_000_000, bytes_accessed=2_000_000, transcendentals=0),
        name="factor",
    )(gram, top)


def mm(left, right, ca=1, cb=0, precision=lax.Precision.HIGH):
    return lax.dot_general(
        left, right, (((ca,), (cb,)), ((), ())), precision=precision, preferred_element_type=jnp.float32
    )


XS, ZS, RS = 4, 8, 8
X_GROUPS = [[z * XS + x for x in range(XS)] for z in range(ZS)]
Z_GROUPS = [[z * XS + x for z in range(ZS)] for x in range(XS)]


def exchange(value, axis, groups=None):
    return lax.all_to_all(value, axis, 0, 0, tiled=True, axis_index_groups=groups)


def to_all(value, count, axis, groups=None):
    return exchange(jnp.broadcast_to(value[None], (count, *value.shape)), axis, groups)


def x_shift(value, k):
    pairs = [(z * XS + x, z * XS + (x + k) % XS) for z in range(ZS) for x in range(XS)]
    return lax.ppermute(value, "col", pairs)


def swap(value):
    cols = ZS * XS
    pairs = [
        (r * cols + z * XS + x, z * cols + r * XS + x)
        for r in range(RS)
        for z in range(ZS)
        for x in range(XS)
    ]
    return lax.ppermute(value, ("row", "col"), pairs)


def gather_x(value):
    shifted = {k: x_shift(value, k) for k in (2, 1, 3)}
    return [value, shifted[1], shifted[2], shifted[3]]


def split(value):
    high = value.astype(jnp.bfloat16)
    return high, (value - high.astype(jnp.float32)).astype(jnp.bfloat16)


def dot_split(left, right):
    def one(a, b):
        return lax.dot_general(a, b, (((1,), (1,)), ((), ())), preferred_element_type=jnp.float32)

    return one(left[0], right[0]) + (one(left[0], right[1]) + one(left[1], right[0]))


def update(x_index, matrix, v_parts, x_parts, v_cols, arrived, inner, t_factor, v_own, x_own):
    rows, cols = matrix.shape
    quarter = rows // XS
    share, piece = NB // RS, cols // RS

    def kernel(at, a_ref, *refs):
        v_refs, x_refs = refs[:XS], refs[XS : 2 * XS]
        vc_ref, got_ref, inner_ref, t_ref, vo_ref, xo_ref, out_ref, w_ref, ys, vs = refs[2 * XS :]
        step = pl.program_id(0)

        @pl.when(step == 0)
        def _():
            core = dot(t_ref[...], inner_ref[...], 0, 0)
            w_ref[...] = xo_ref[...] - 0.5 * dot(vo_ref[...], core)
            even = split(0.5 * (core + core.T))
            vs[0], vs[1] = split(vc_ref[...])
            change = dot_split((vs[0], vs[1]), even)
            for r in range(RS):
                at_rows = slice(r * piece, (r + 1) * piece)
                ys[0, at_rows], ys[1, at_rows] = split(got_ref[r, share:] - change[at_rows])

        for j in range(XS):

            @pl.when(step == j)
            def _(j=j):
                out = a_ref[...] - dot_split(split(v_refs[j][...]), (ys[0], ys[1]))
                out_ref[...] = out - dot_split(split(x_refs[j][...]), (vs[0], vs[1]))

    def whole(array):
        return pl.BlockSpec(array.shape, lambda j, at: (0,) * array.ndim)

    block = pl.BlockSpec((quarter, cols), lambda j, at: ((at[0] + XS - j) % XS, 0))
    others = [*v_parts, *x_parts, v_cols, arrived, inner, t_factor, v_own, x_own]
    return pl.pallas_call(
        kernel,
        grid_spec=pltpu.PrefetchScalarGridSpec(
            num_scalar_prefetch=1,
            grid=(XS,),
            in_specs=[block] + [whole(array) for array in others],
            out_specs=[block, whole(x_own)],
            scratch_shapes=[pltpu.VMEM((2, cols, NB), jnp.bfloat16)] * 2,
        ),
        out_shape=[
            jax.ShapeDtypeStruct((rows, cols), jnp.float32),
            jax.ShapeDtypeStruct(x_own.shape, jnp.float32),
        ],
        compiler_params=pltpu.CompilerParams(vmem_limit_bytes=32 * 1024 * 1024),
        cost_estimate=pl.CostEstimate(flops=6_000_000_000, bytes_accessed=16_000_000, transcendentals=0),
        name="update",
    )(x_index[None], matrix, *others)


def body(matrix):
    rows, cols = matrix.shape
    row_index = lax.axis_index("row")
    col_index = lax.axis_index("col")
    z_index, x_index = col_index // XS, col_index % XS
    piece = cols // RS
    quarter = rows // XS
    share = NB // RS

    turned = matrix[: 2 * NB, :].T
    col_ids = col_index * cols + jnp.arange(cols)
    strip_turned = jnp.where((col_ids >= NB)[:, None], turned[:, :NB], 0.0)
    pieces = jnp.concatenate(
        [strip_turned.reshape(RS, piece, NB), turned[:, NB:].reshape(RS, piece, NB)], axis=1
    )
    pieces = exchange(pieces, "row")[0]
    strip_piece = pieces[:piece]
    strip_cols = to_all(strip_piece, RS, "row").reshape(cols, NB)
    pieces = swap(pieces)
    strip_moved, next_piece = pieces[:piece], pieces[piece:]

    own_cols = lax.dynamic_slice_in_dim(strip_cols, row_index * share, share, 1)
    gram_share = mm(own_cols, strip_cols, 0, 0, HI)
    top_share = lax.dynamic_slice_in_dim(strip_cols, NB + row_index * share, share, 0)
    small = jnp.concatenate([gram_share, jnp.where(col_index == 0, top_share, 0.0)], axis=0)
    small = jnp.sum(to_all(small, XS, "col", X_GROUPS), axis=0)
    small = jnp.sum(to_all(small, ZS, "col", Z_GROUPS), axis=0)
    small = to_all(small, RS, "row")
    gram_sum = small[:, :share].reshape(NB, NB)
    top_block = small[:, share:].reshape(NB, NB)
    low, up, low_inv, to_v, to_x, sign = factor_all(gram_sum, top_block)

    def partial(k):
        start = (x_index + k) % XS * quarter
        return mm(lax.dynamic_slice_in_dim(matrix, start, quarter, 0), strip_cols)

    prod = x_shift(partial(2), 2) + x_shift(partial(1), 1) + x_shift(partial(3), 3) + partial(0)
    both = jnp.concatenate(
        [prod.reshape(ZS, piece, NB), jnp.broadcast_to(strip_moved[None], (ZS, piece, NB))], axis=1
    )
    both = exchange(both, "col", Z_GROUPS)
    prod = jnp.sum(both[:, :piece], axis=0)
    strip_some = both[:, piece:].reshape(quarter, NB)
    strip_parts = gather_x(strip_some)

    x_piece = mm(mm(prod, to_x, 1, 0, HI) + next_piece, low_inv, 1, 1, HI)
    x_moved = swap(x_piece)
    x_some = to_all(x_piece, ZS, "col", Z_GROUPS).reshape(quarter, NB)
    x_parts = gather_x(x_some)

    low_placed = jnp.concatenate([jnp.zeros((quarter - NB, NB), jnp.float32), low], axis=0)
    late = (jnp.arange(quarter) >= quarter - NB)[:, None]

    def reflectors(strip, holds_top):
        return jnp.where(late & holds_top, low_placed, mm(strip, to_v))

    v_parts = [
        reflectors(part, (row_index == 0) & (x_index == k)) for k, part in enumerate(strip_parts)
    ]
    v_cols = reflectors(strip_cols, col_index == 0)
    inner = mm(lax.dynamic_slice_in_dim(v_parts[0], z_index * share, share, 1), x_some, 0, 0)
    inner = jnp.sum(to_all(inner, XS, "col", X_GROUPS), axis=0)
    arrived = to_all(jnp.concatenate([inner, x_moved], axis=0), RS, "row")
    inner = jnp.sum(arrived[:, :share], axis=0)
    inner = to_all(inner, ZS, "col", Z_GROUPS).reshape(NB, NB)
    t_factor = mm(up * sign, low_inv, 1, 1, HI)

    out_rows = rows // (XS * ZS)
    out_start = col_index * out_rows
    mine = (x_index + XS - out_start // quarter) % XS

    def own(parts):
        cut = [lax.dynamic_slice_in_dim(part, out_start % quarter, out_rows, 0) for part in parts]
        return jnp.where(mine < 2, jnp.where(mine == 0, cut[0], cut[1]), jnp.where(mine == 2, cut[2], cut[3]))

    v_own = own(v_parts)
    updated, w_own = update(
        x_index, matrix, v_parts, x_parts, v_cols, arrived, inner, t_factor, v_own, own(x_parts)
    )
    return (updated, v_own[None], w_own[None])


def solution(mesh):
    return jax.shard_map(
        body,
        mesh=mesh,
        in_specs=(P("row", "col"),),
        out_specs=(P("row", "col"), P(None, ("row", "col"), None), P(None, ("row", "col"), None)),
        check_vma=False,
    )
```

```python
import jax
import jax.numpy as jnp
from jax import lax
from jax.experimental import pallas as pl
from jax.experimental.pallas import tpu as pltpu
from jax.sharding import PartitionSpec as P

HI = lax.Precision.HIGHEST
NB = 256
BK = 64
STEPS = NB // BK
LOOK = 8


def dot(a, b, ca=1, cb=0):
    return lax.dot_general(a, b, (((ca,), (cb,)), ((), ())), precision=HI, preferred_element_type=jnp.float32)


def lanes_of(chunk, k):
    return jnp.broadcast_to(chunk[:, k : k + 1], chunk.shape)


def leaf_start(block, below):
    eye = jnp.eye(BK, dtype=jnp.float32)
    top = jnp.concatenate([block, eye], axis=1)
    rows = [top[8 * i : 8 * i + 8] for i in range(BK // 8)]
    if below:
        low = jnp.concatenate([eye, jnp.zeros((BK, BK), jnp.float32)], axis=1)
        rows += [low[8 * i : 8 * i + 8] for i in range(BK // 8)]
    return {"rows": rows, "below": below, "recip": [], "sign": [], "pivot": []}


def leaf_group(state, first, look, signed):
    rows = state["rows"]
    half = BK // 8
    lane = lax.broadcasted_iota(jnp.int32, (1, 2 * BK), 1)
    sub = lax.broadcasted_iota(jnp.int32, (8, 2 * BK), 0)
    active = list(range(first // 8, half))
    if state["below"]:
        active += list(range(half, half + (first + look - 1) // 8 + 1))
    cols = [{i: lanes_of(rows[i], first + j) for i in active} for j in range(look)]
    for j in range(look):
        k = first + j
        own, off = k // 8, k % 8
        pivot = cols[j][own][off : off + 1]
        if signed:
            sign = jnp.where(pivot >= 0, 1.0, -1.0).astype(jnp.float32)
            pivot = pivot + sign
            state["sign"].append(sign)
        recip = 1.0 / pivot
        state["recip"].append(recip)
        state["pivot"].append(pivot)
        scaled = jnp.where(lane > k, rows[own][off : off + 1] * recip, 0.0)
        ahead = [cols[jj][own][off : off + 1] * recip for jj in range(j + 1, look)]
        for i in active:
            if i < half and i == own:
                if off == 7:
                    continue
                mult = jnp.where(sub > off, cols[j][i], 0.0)
            else:
                mult = cols[j][i]
            rows[i] = rows[i] - mult * scaled
            for n, jj in enumerate(range(j + 1, look)):
                cols[jj][i] = cols[jj][i] - mult * ahead[n]


def pick(rows):
    lane = lax.broadcasted_iota(jnp.int32, (1, 2 * BK), 1)
    out = jnp.zeros((1, 2 * BK), jnp.float32)
    for k, row in enumerate(rows):
        out = jnp.where(lane == k, row, out)
    return out[:, :BK]


def factor_step(p, refs):
    h_ref, l_ref, u_ref, li_ref, ui_ref, s_ref, y_ref = refs
    chol = lu = None
    if p < STEPS:
        chol = leaf_start(h_ref[p * BK : (p + 1) * BK, p * BK : (p + 1) * BK], False)
    if p > 0:
        lu = leaf_start(y_ref[(p - 1) * BK : p * BK, :], True)
    for first in range(0, BK, LOOK):
        if chol is not None:
            leaf_group(chol, first, LOOK, False)
        if lu is not None:
            leaf_group(lu, first, LOOK, True)
    tri_r = lax.broadcasted_iota(jnp.int32, (BK, BK), 0)
    tri_c = lax.broadcasted_iota(jnp.int32, (BK, BK), 1)
    half = BK // 8
    if chol is not None:
        inv_low = jnp.concatenate(chol["rows"], axis=0)[:, BK:]
        recip = pick(chol["recip"])
        scale = jnp.sqrt(recip)
        panel = dot(h_ref[:, p * BK : (p + 1) * BK], inv_low, 1, 1) * scale
        h_ref[:, p * BK : (p + 1) * BK] = panel
        if p + 1 < STEPS:
            after = panel[(p + 1) * BK : NB]
            h_ref[:, (p + 1) * BK :] = h_ref[:, (p + 1) * BK :] - dot(panel, after, 1, 1)
    if lu is not None:
        q0, q1 = (p - 1) * BK, p * BK
        full = jnp.concatenate(lu["rows"][:half], axis=0)
        low_inv = full[:, BK:]
        recip = pick(lu["recip"])
        pivot = pick(lu["pivot"])
        s_ref[:, q0:q1] = pick(lu["sign"])
        main = full[:, :BK]
        l_diag = jnp.where(tri_r > tri_c, main * recip, jnp.where(tri_r == tri_c, 1.0, 0.0))
        u_diag = jnp.where(tri_r < tri_c, main, jnp.where(tri_r == tri_c, pivot, 0.0))
        low = jnp.concatenate(lu["rows"][half:], axis=0)[:, :BK]
        u_inv = jnp.where(tri_r <= tri_c, low * recip, 0.0)
        l_ref[q0:q1, q0:q1] = l_diag
        u_ref[q0:q1, q0:q1] = u_diag
        li_ref[q0:q1, q0:q1] = low_inv
        ui_ref[q0:q1, q0:q1] = u_inv
        if p < STEPS:
            l_ref[q1:, q0:q1] = dot(y_ref[q1:, :], u_inv)
        if p > 1:
            li_ref[q0:q1, :q0] = -dot(low_inv, dot(l_ref[q0:q1, :q0], li_ref[:q0, :q0]))
            ui_ref[:q0, q0:q1] = -dot(ui_ref[:q0, :q0], dot(u_ref[:q0, q0:q1], u_inv))
    if p < STEPS:
        q1 = p * BK
        col = h_ref[NB : 2 * NB, p * BK : (p + 1) * BK]
        if p > 0:
            upper = dot(li_ref[:q1, :q1], col[:q1])
            u_ref[:q1, q1 : q1 + BK] = upper
            y_ref[q1:, :] = col[q1:] - dot(l_ref[q1:, :q1], upper)
        else:
            y_ref[...] = col


def factor_all(gram, top):
    def kernel(g_ref, c_ref, l_out, u_out, li_out, m_out, ri_out, s_out, h, y, ui):
        h[:NB] = g_ref[...]
        h[NB : 2 * NB] = c_ref[...]
        r = lax.broadcasted_iota(jnp.int32, (NB, NB), 0)
        c = lax.broadcasted_iota(jnp.int32, (NB, NB), 1)
        h[2 * NB :] = jnp.where(r == c, 1.0, 0.0).astype(jnp.float32)
        for ref in (l_out, u_out, li_out, ui):
            ref[...] = jnp.zeros((NB, NB), jnp.float32)
        for p in range(STEPS + 1):
            factor_step(p, (h, l_out, u_out, li_out, ui, s_out, y))
        r_inv = h[2 * NB :]
        m_out[...] = dot(r_inv, ui[...])
        ri_out[...] = r_inv * s_out[...]

    sq = jax.ShapeDtypeStruct((NB, NB), jnp.float32)
    return pl.pallas_call(
        kernel,
        out_shape=[sq, sq, sq, sq, sq, jax.ShapeDtypeStruct((1, NB), jnp.float32)],
        scratch_shapes=[
            pltpu.VMEM((3 * NB, NB), jnp.float32),
            pltpu.VMEM((NB, BK), jnp.float32),
            pltpu.VMEM((NB, NB), jnp.float32),
        ],
        compiler_params=pltpu.CompilerParams(vmem_limit_bytes=24 * 1024 * 1024),
        cost_estimate=pl.CostEstimate(flops=20_000_000_000, bytes_accessed=2_000_000, transcendentals=0),
        name="factor",
    )(gram, top)


def mm(left, right, ca=1, cb=0, precision=lax.Precision.HIGH):
    return lax.dot_general(
        left, right, (((ca,), (cb,)), ((), ())), precision=precision, preferred_element_type=jnp.float32
    )


XS, ZS, RS = 4, 8, 8
X_GROUPS = [[z * XS + x for x in range(XS)] for z in range(ZS)]
Z_GROUPS = [[z * XS + x for z in range(ZS)] for x in range(XS)]


def exchange(value, axis, groups=None):
    return lax.all_to_all(value, axis, 0, 0, tiled=True, axis_index_groups=groups)


def to_all(value, count, axis, groups=None):
    return exchange(jnp.broadcast_to(value[None], (count, *value.shape)), axis, groups)


def x_shift(value, k):
    pairs = [(z * XS + x, z * XS + (x + k) % XS) for z in range(ZS) for x in range(XS)]
    return lax.ppermute(value, "col", pairs)


def swap(value):
    cols = ZS * XS
    pairs = [
        (r * cols + z * XS + x, z * cols + r * XS + x)
        for r in range(RS)
        for z in range(ZS)
        for x in range(XS)
    ]
    return lax.ppermute(value, ("row", "col"), pairs)


def gather_x(value):
    shifted = {k: x_shift(value, k) for k in (2, 1, 3)}
    return [value, shifted[1], shifted[2], shifted[3]]


def split(value):
    high = value.astype(jnp.bfloat16)
    return high, (value - high.astype(jnp.float32)).astype(jnp.bfloat16)


def dot_split(left, right):
    def one(a, b):
        return lax.dot_general(a, b, (((1,), (1,)), ((), ())), preferred_element_type=jnp.float32)

    return one(left[0], right[0]) + (one(left[0], right[1]) + one(left[1], right[0]))


def update(x_index, matrix, v_parts, x_parts, v_cols, arrived, inner, t_factor, v_own, x_own):
    rows, cols = matrix.shape
    quarter = rows // XS
    share, piece = NB // RS, cols // RS

    def kernel(at, a_ref, *refs):
        v_refs, x_refs = refs[:XS], refs[XS : 2 * XS]
        vc_ref, got_ref, inner_ref, t_ref, vo_ref, xo_ref, out_ref, w_ref, ys, vs = refs[2 * XS :]
        step = pl.program_id(0)

        @pl.when(step == 0)
        def _():
            core = dot(t_ref[...], inner_ref[...], 0, 0)
            w_ref[...] = xo_ref[...] - 0.5 * dot(vo_ref[...], core)
            even = split(0.5 * (core + core.T))
            vs[0], vs[1] = split(vc_ref[...])
            change = dot_split((vs[0], vs[1]), even)
            for r in range(RS):
                at_rows = slice(r * piece, (r + 1) * piece)
                ys[0, at_rows], ys[1, at_rows] = split(got_ref[r, share:] - change[at_rows])

        for j in range(XS):

            @pl.when(step == j)
            def _(j=j):
                out = a_ref[...] - dot_split(split(v_refs[j][...]), (ys[0], ys[1]))
                out_ref[...] = out - dot_split(split(x_refs[j][...]), (vs[0], vs[1]))

    def whole(array):
        return pl.BlockSpec(array.shape, lambda j, at: (0,) * array.ndim)

    block = pl.BlockSpec((quarter, cols), lambda j, at: ((at[0] + XS - j) % XS, 0))
    others = [*v_parts, *x_parts, v_cols, arrived, inner, t_factor, v_own, x_own]
    return pl.pallas_call(
        kernel,
        grid_spec=pltpu.PrefetchScalarGridSpec(
            num_scalar_prefetch=1,
            grid=(XS,),
            in_specs=[block] + [whole(array) for array in others],
            out_specs=[block, whole(x_own)],
            scratch_shapes=[pltpu.VMEM((2, cols, NB), jnp.bfloat16)] * 2,
        ),
        out_shape=[
            jax.ShapeDtypeStruct((rows, cols), jnp.float32),
            jax.ShapeDtypeStruct(x_own.shape, jnp.float32),
        ],
        compiler_params=pltpu.CompilerParams(vmem_limit_bytes=56 * 1024 * 1024),
        cost_estimate=pl.CostEstimate(flops=6_000_000_000, bytes_accessed=16_000_000, transcendentals=0),
        name="update",
    )(x_index[None], matrix, *others)


def body(matrix):
    rows, cols = matrix.shape
    row_index = lax.axis_index("row")
    col_index = lax.axis_index("col")
    z_index, x_index = col_index // XS, col_index % XS
    piece = cols // RS
    quarter = rows // XS
    share = NB // RS

    turned = matrix[: 2 * NB, :].T
    col_ids = col_index * cols + jnp.arange(cols)
    strip_turned = jnp.where((col_ids >= NB)[:, None], turned[:, :NB], 0.0)
    pieces = jnp.concatenate(
        [strip_turned.reshape(RS, piece, NB), turned[:, NB:].reshape(RS, piece, NB)], axis=1
    )
    pieces = exchange(pieces, "row")[0]
    strip_piece = pieces[:piece]
    strip_cols = lax.all_gather(strip_piece, "row", axis=0, tiled=True)
    pieces = swap(pieces)
    strip_moved, next_piece = pieces[:piece], pieces[piece:]

    own_cols = lax.dynamic_slice_in_dim(strip_cols, row_index * share, share, 1)
    gram_share = mm(own_cols, strip_cols, 0, 0, HI)
    top_share = lax.dynamic_slice_in_dim(strip_cols, NB + row_index * share, share, 0)
    small = jnp.concatenate([gram_share, jnp.where(col_index == 0, top_share, 0.0)], axis=0)
    small = jnp.sum(to_all(small, XS, "col", X_GROUPS), axis=0)
    small = jnp.sum(to_all(small, ZS, "col", Z_GROUPS), axis=0)
    small = to_all(small, RS, "row")
    gram_sum = small[:, :share].reshape(NB, NB)
    top_block = small[:, share:].reshape(NB, NB)
    low, up, low_inv, to_v, to_x, sign = factor_all(gram_sum, top_block)

    def partial(k):
        start = (x_index + k) % XS * quarter
        return mm(lax.dynamic_slice_in_dim(matrix, start, quarter, 0), strip_cols)

    prod = x_shift(partial(2), 2) + x_shift(partial(1), 1) + x_shift(partial(3), 3) + partial(0)
    both = jnp.concatenate(
        [prod.reshape(ZS, piece, NB), jnp.broadcast_to(strip_moved[None], (ZS, piece, NB))], axis=1
    )
    both = exchange(both, "col", Z_GROUPS)
    prod = jnp.sum(both[:, :piece], axis=0)
    strip_some = both[:, piece:].reshape(quarter, NB)
    strip_parts = gather_x(strip_some)

    x_piece = mm(mm(prod, to_x, 1, 0, HI) + next_piece, low_inv, 1, 1, HI)
    x_moved = swap(x_piece)
    x_some = to_all(x_piece, ZS, "col", Z_GROUPS).reshape(quarter, NB)
    x_parts = gather_x(x_some)

    low_placed = jnp.concatenate([jnp.zeros((quarter - NB, NB), jnp.float32), low], axis=0)
    late = (jnp.arange(quarter) >= quarter - NB)[:, None]

    def reflectors(strip, holds_top):
        return jnp.where(late & holds_top, low_placed, mm(strip, to_v))

    v_parts = [
        reflectors(part, (row_index == 0) & (x_index == k)) for k, part in enumerate(strip_parts)
    ]
    v_cols = reflectors(strip_cols, col_index == 0)
    inner = mm(lax.dynamic_slice_in_dim(v_parts[0], z_index * share, share, 1), x_some, 0, 0)
    inner = jnp.sum(to_all(inner, XS, "col", X_GROUPS), axis=0)
    arrived = to_all(jnp.concatenate([inner, x_moved], axis=0), RS, "row")
    inner = jnp.sum(arrived[:, :share], axis=0)
    inner = to_all(inner, ZS, "col", Z_GROUPS).reshape(NB, NB)
    t_factor = mm(up * sign, low_inv, 1, 1, HI)

    out_rows = rows // (XS * ZS)
    out_start = col_index * out_rows
    mine = (x_index + XS - out_start // quarter) % XS

    def own(parts):
        cut = [lax.dynamic_slice_in_dim(part, out_start % quarter, out_rows, 0) for part in parts]
        return jnp.where(mine < 2, jnp.where(mine == 0, cut[0], cut[1]), jnp.where(mine == 2, cut[2], cut[3]))

    v_own = own(v_parts)
    updated, w_own = update(
        x_index, matrix, v_parts, x_parts, v_cols, arrived, inner, t_factor, v_own, own(x_parts)
    )
    return (updated, v_own[None], w_own[None])


def solution(mesh):
    return jax.shard_map(
        body,
        mesh=mesh,
        in_specs=(P("row", "col"),),
        out_specs=(P("row", "col"), P(None, ("row", "col"), None), P(None, ("row", "col"), None)),
        check_vma=False,
    )
```

```python
import jax
import jax.numpy as jnp
from jax import lax
from jax.experimental import pallas as pl
from jax.experimental.pallas import tpu as pltpu
from jax.sharding import PartitionSpec as P

HI = lax.Precision.HIGHEST
NB = 256
BK = 64
STEPS = NB // BK
LOOK = 8


def dot(a, b, ca=1, cb=0):
    return lax.dot_general(a, b, (((ca,), (cb,)), ((), ())), precision=HI, preferred_element_type=jnp.float32)


def lanes_of(chunk, k):
    return jnp.broadcast_to(chunk[:, k : k + 1], chunk.shape)


def leaf_start(block, below):
    eye = jnp.eye(BK, dtype=jnp.float32)
    top = jnp.concatenate([block, eye], axis=1)
    rows = [top[8 * i : 8 * i + 8] for i in range(BK // 8)]
    if below:
        low = jnp.concatenate([eye, jnp.zeros((BK, BK), jnp.float32)], axis=1)
        rows += [low[8 * i : 8 * i + 8] for i in range(BK // 8)]
    return {"rows": rows, "below": below, "recip": [], "sign": [], "pivot": []}


def leaf_group(state, first, look, signed):
    rows = state["rows"]
    half = BK // 8
    lane = lax.broadcasted_iota(jnp.int32, (1, 2 * BK), 1)
    sub = lax.broadcasted_iota(jnp.int32, (8, 2 * BK), 0)
    active = list(range(first // 8, half))
    if state["below"]:
        active += list(range(half, half + (first + look - 1) // 8 + 1))
    cols = [{i: lanes_of(rows[i], first + j) for i in active} for j in range(look)]
    for j in range(look):
        k = first + j
        own, off = k // 8, k % 8
        pivot = cols[j][own][off : off + 1]
        if signed:
            sign = jnp.where(pivot >= 0, 1.0, -1.0).astype(jnp.float32)
            pivot = pivot + sign
            state["sign"].append(sign)
        recip = 1.0 / pivot
        state["recip"].append(recip)
        state["pivot"].append(pivot)
        scaled = jnp.where(lane > k, rows[own][off : off + 1] * recip, 0.0)
        ahead = [cols[jj][own][off : off + 1] * recip for jj in range(j + 1, look)]
        for i in active:
            if i < half and i == own:
                if off == 7:
                    continue
                mult = jnp.where(sub > off, cols[j][i], 0.0)
            else:
                mult = cols[j][i]
            rows[i] = rows[i] - mult * scaled
            for n, jj in enumerate(range(j + 1, look)):
                cols[jj][i] = cols[jj][i] - mult * ahead[n]


def pick(rows):
    lane = lax.broadcasted_iota(jnp.int32, (1, 2 * BK), 1)
    out = jnp.zeros((1, 2 * BK), jnp.float32)
    for k, row in enumerate(rows):
        out = jnp.where(lane == k, row, out)
    return out[:, :BK]


def factor_step(p, refs):
    h_ref, l_ref, u_ref, li_ref, ui_ref, s_ref, y_ref = refs
    chol = lu = None
    if p < STEPS:
        chol = leaf_start(h_ref[p * BK : (p + 1) * BK, p * BK : (p + 1) * BK], False)
    if p > 0:
        lu = leaf_start(y_ref[(p - 1) * BK : p * BK, :], True)
    for first in range(0, BK, LOOK):
        if chol is not None:
            leaf_group(chol, first, LOOK, False)
        if lu is not None:
            leaf_group(lu, first, LOOK, True)
    tri_r = lax.broadcasted_iota(jnp.int32, (BK, BK), 0)
    tri_c = lax.broadcasted_iota(jnp.int32, (BK, BK), 1)
    half = BK // 8
    if chol is not None:
        inv_low = jnp.concatenate(chol["rows"], axis=0)[:, BK:]
        recip = pick(chol["recip"])
        scale = jnp.sqrt(recip)
        panel = dot(h_ref[:, p * BK : (p + 1) * BK], inv_low, 1, 1) * scale
        h_ref[:, p * BK : (p + 1) * BK] = panel
        if p + 1 < STEPS:
            after = panel[(p + 1) * BK : NB]
            h_ref[:, (p + 1) * BK :] = h_ref[:, (p + 1) * BK :] - dot(panel, after, 1, 1)
    if lu is not None:
        q0, q1 = (p - 1) * BK, p * BK
        full = jnp.concatenate(lu["rows"][:half], axis=0)
        low_inv = full[:, BK:]
        recip = pick(lu["recip"])
        pivot = pick(lu["pivot"])
        s_ref[:, q0:q1] = pick(lu["sign"])
        main = full[:, :BK]
        l_diag = jnp.where(tri_r > tri_c, main * recip, jnp.where(tri_r == tri_c, 1.0, 0.0))
        u_diag = jnp.where(tri_r < tri_c, main, jnp.where(tri_r == tri_c, pivot, 0.0))
        low = jnp.concatenate(lu["rows"][half:], axis=0)[:, :BK]
        u_inv = jnp.where(tri_r <= tri_c, low * recip, 0.0)
        l_ref[q0:q1, q0:q1] = l_diag
        u_ref[q0:q1, q0:q1] = u_diag
        li_ref[q0:q1, q0:q1] = low_inv
        ui_ref[q0:q1, q0:q1] = u_inv
        if p < STEPS:
            l_ref[q1:, q0:q1] = dot(y_ref[q1:, :], u_inv)
        if p > 1:
            li_ref[q0:q1, :q0] = -dot(low_inv, dot(l_ref[q0:q1, :q0], li_ref[:q0, :q0]))
            ui_ref[:q0, q0:q1] = -dot(ui_ref[:q0, :q0], dot(u_ref[:q0, q0:q1], u_inv))
    if p < STEPS:
        q1 = p * BK
        col = h_ref[NB : 2 * NB, p * BK : (p + 1) * BK]
        if p > 0:
            upper = dot(li_ref[:q1, :q1], col[:q1])
            u_ref[:q1, q1 : q1 + BK] = upper
            y_ref[q1:, :] = col[q1:] - dot(l_ref[q1:, :q1], upper)
        else:
            y_ref[...] = col


def factor_all(gram, top):
    def kernel(g_ref, c_ref, l_out, u_out, li_out, m_out, ri_out, s_out, h, y, ui):
        h[:NB] = g_ref[...]
        h[NB : 2 * NB] = c_ref[...]
        r = lax.broadcasted_iota(jnp.int32, (NB, NB), 0)
        c = lax.broadcasted_iota(jnp.int32, (NB, NB), 1)
        h[2 * NB :] = jnp.where(r == c, 1.0, 0.0).astype(jnp.float32)
        for ref in (l_out, u_out, li_out, ui):
            ref[...] = jnp.zeros((NB, NB), jnp.float32)
        for p in range(STEPS + 1):
            factor_step(p, (h, l_out, u_out, li_out, ui, s_out, y))
        r_inv = h[2 * NB :]
        m_out[...] = dot(r_inv, ui[...])
        ri_out[...] = r_inv * s_out[...]

    sq = jax.ShapeDtypeStruct((NB, NB), jnp.float32)
    return pl.pallas_call(
        kernel,
        out_shape=[sq, sq, sq, sq, sq, jax.ShapeDtypeStruct((1, NB), jnp.float32)],
        scratch_shapes=[
            pltpu.VMEM((3 * NB, NB), jnp.float32),
            pltpu.VMEM((NB, BK), jnp.float32),
            pltpu.VMEM((NB, NB), jnp.float32),
        ],
        compiler_params=pltpu.CompilerParams(vmem_limit_bytes=24 * 1024 * 1024),
        cost_estimate=pl.CostEstimate(flops=20_000_000_000, bytes_accessed=2_000_000, transcendentals=0),
        name="factor",
    )(gram, top)


def mm(left, right, ca=1, cb=0, precision=lax.Precision.HIGH):
    return lax.dot_general(
        left, right, (((ca,), (cb,)), ((), ())), precision=precision, preferred_element_type=jnp.float32
    )


XS, ZS, RS = 4, 8, 8
X_GROUPS = [[z * XS + x for x in range(XS)] for z in range(ZS)]
Z_GROUPS = [[z * XS + x for z in range(ZS)] for x in range(XS)]


def exchange(value, axis, groups=None):
    return lax.all_to_all(value, axis, 0, 0, tiled=True, axis_index_groups=groups)


def to_all(value, count, axis, groups=None):
    return exchange(jnp.broadcast_to(value[None], (count, *value.shape)), axis, groups)


def x_shift(value, k):
    pairs = [(z * XS + x, z * XS + (x + k) % XS) for z in range(ZS) for x in range(XS)]
    return lax.ppermute(value, "col", pairs)


def swap(value):
    cols = ZS * XS
    pairs = [
        (r * cols + z * XS + x, z * cols + r * XS + x)
        for r in range(RS)
        for z in range(ZS)
        for x in range(XS)
    ]
    return lax.ppermute(value, ("row", "col"), pairs)


def gather_x(value):
    shifted = {k: x_shift(value, k) for k in (2, 1, 3)}
    return [value, shifted[1], shifted[2], shifted[3]]


def split(value):
    high = value.astype(jnp.bfloat16)
    return high, (value - high.astype(jnp.float32)).astype(jnp.bfloat16)


def dot_split(left, right):
    def one(a, b):
        return lax.dot_general(a, b, (((1,), (1,)), ((), ())), preferred_element_type=jnp.float32)

    return one(left[0], right[0]) + (one(left[0], right[1]) + one(left[1], right[0]))


def update(places, out_rows, matrix, v_parts, x_parts, v_cols, arrived, inner, t_factor):
    rows, cols = matrix.shape
    quarter = rows // XS
    share, piece = NB // RS, cols // RS

    def kernel(at, a_ref, *refs):
        v_refs, x_refs = refs[:XS], refs[XS : 2 * XS]
        vc_ref, got_ref, inner_ref, t_ref, out_ref, v_ref, w_ref, ys, vs, core_ref = refs[2 * XS :]
        step = pl.program_id(0)

        @pl.when(step == 0)
        def _():
            core = dot(t_ref[...], inner_ref[...], 0, 0)
            core_ref[...] = core
            even = split(0.5 * (core + core.T))
            vs[0], vs[1] = split(vc_ref[...])
            change = dot_split((vs[0], vs[1]), even)
            for r in range(RS):
                at_rows = slice(r * piece, (r + 1) * piece)
                ys[0, at_rows], ys[1, at_rows] = split(got_ref[r, share:] - change[at_rows])

        for j in range(XS):

            @pl.when(step == j)
            def _(j=j):
                out = a_ref[...] - dot_split(split(v_refs[j][...]), (ys[0], ys[1]))
                out_ref[...] = out - dot_split(split(x_refs[j][...]), (vs[0], vs[1]))

            @pl.when((step == j) & (at[1] == j))
            def _(j=j):
                mine = pl.ds(pl.multiple_of(at[2], out_rows), out_rows)
                v_ref[...] = v_refs[j][mine]
                w_ref[...] = x_refs[j][mine] - 0.5 * dot(v_refs[j][mine], core_ref[...])

    def whole(array):
        return pl.BlockSpec(array.shape, lambda j, at: (0,) * array.ndim)

    block = pl.BlockSpec((quarter, cols), lambda j, at: ((at[0] + XS - j) % XS, 0))
    others = [*v_parts, *x_parts, v_cols, arrived, inner, t_factor]
    own = jax.ShapeDtypeStruct((out_rows, NB), jnp.float32)
    return pl.pallas_call(
        kernel,
        grid_spec=pltpu.PrefetchScalarGridSpec(
            num_scalar_prefetch=1,
            grid=(XS,),
            in_specs=[block] + [whole(array) for array in others],
            out_specs=[block, whole(own), whole(own)],
            scratch_shapes=[pltpu.VMEM((2, cols, NB), jnp.bfloat16)] * 2
            + [pltpu.VMEM((NB, NB), jnp.float32)],
        ),
        out_shape=[
            jax.ShapeDtypeStruct((rows, cols), jnp.float32),
            own,
            own,
        ],
        compiler_params=pltpu.CompilerParams(vmem_limit_bytes=56 * 1024 * 1024),
        cost_estimate=pl.CostEstimate(flops=6_000_000_000, bytes_accessed=16_000_000, transcendentals=0),
        name="update",
    )(places, matrix, *others)


def body(matrix):
    rows, cols = matrix.shape
    row_index = lax.axis_index("row")
    col_index = lax.axis_index("col")
    z_index, x_index = col_index // XS, col_index % XS
    piece = cols // RS
    quarter = rows // XS
    share = NB // RS

    turned = matrix[: 2 * NB, :].T
    col_ids = col_index * cols + jnp.arange(cols)
    strip_turned = jnp.where((col_ids >= NB)[:, None], turned[:, :NB], 0.0)
    pieces = jnp.concatenate(
        [strip_turned.reshape(RS, piece, NB), turned[:, NB:].reshape(RS, piece, NB)], axis=1
    )
    pieces = exchange(pieces, "row")[0]
    strip_piece = pieces[:piece]
    strip_cols = lax.all_gather(strip_piece, "row", axis=0, tiled=True)
    pieces = swap(pieces)
    strip_moved, next_piece = pieces[:piece], pieces[piece:]

    own_cols = lax.dynamic_slice_in_dim(strip_cols, row_index * share, share, 1)
    gram_share = mm(own_cols, strip_cols, 0, 0, HI)
    top_share = lax.dynamic_slice_in_dim(strip_cols, NB + row_index * share, share, 0)
    small = jnp.concatenate([gram_share, jnp.where(col_index == 0, top_share, 0.0)], axis=0)
    small = jnp.sum(to_all(small, XS, "col", X_GROUPS), axis=0)
    small = jnp.sum(to_all(small, ZS, "col", Z_GROUPS), axis=0)
    small = to_all(small, RS, "row")
    gram_sum = small[:, :share].reshape(NB, NB)
    top_block = small[:, share:].reshape(NB, NB)
    low, up, low_inv, to_v, to_x, sign = factor_all(gram_sum, top_block)

    def partial(k):
        start = (x_index + k) % XS * quarter
        return mm(lax.dynamic_slice_in_dim(matrix, start, quarter, 0), strip_cols)

    prod = x_shift(partial(2), 2) + x_shift(partial(1), 1) + x_shift(partial(3), 3) + partial(0)
    both = jnp.concatenate(
        [prod.reshape(ZS, piece, NB), jnp.broadcast_to(strip_moved[None], (ZS, piece, NB))], axis=1
    )
    both = exchange(both, "col", Z_GROUPS)
    prod = jnp.sum(both[:, :piece], axis=0)
    strip_some = both[:, piece:].reshape(quarter, NB)
    strip_parts = gather_x(strip_some)

    x_piece = mm(mm(prod, to_x, 1, 0, HI) + next_piece, low_inv, 1, 1, HI)
    x_moved = swap(x_piece)
    x_some = to_all(x_piece, ZS, "col", Z_GROUPS).reshape(quarter, NB)
    x_parts = gather_x(x_some)

    low_placed = jnp.concatenate([jnp.zeros((quarter - NB, NB), jnp.float32), low], axis=0)
    late = (jnp.arange(quarter) >= quarter - NB)[:, None]

    def reflectors(strip, holds_top):
        return jnp.where(late & holds_top, low_placed, mm(strip, to_v))

    v_parts = [
        reflectors(part, (row_index == 0) & (x_index == k)) for k, part in enumerate(strip_parts)
    ]
    v_cols = reflectors(strip_cols, col_index == 0)
    inner = mm(lax.dynamic_slice_in_dim(v_parts[0], z_index * share, share, 1), x_some, 0, 0)
    inner = jnp.sum(to_all(inner, XS, "col", X_GROUPS), axis=0)
    arrived = to_all(jnp.concatenate([inner, x_moved], axis=0), RS, "row")
    inner = jnp.sum(arrived[:, :share], axis=0)
    inner = to_all(inner, ZS, "col", Z_GROUPS).reshape(NB, NB)
    t_factor = mm(up * sign, low_inv, 1, 1, HI)

    out_rows = rows // (XS * ZS)
    out_start = col_index * out_rows
    mine = (x_index + XS - out_start // quarter) % XS

    places = jnp.stack([x_index, mine, out_start % quarter])
    updated, v_own, w_own = update(
        places, out_rows, matrix, v_parts, x_parts, v_cols, arrived, inner, t_factor
    )
    return (updated, v_own[None], w_own[None])


def solution(mesh):
    return jax.shard_map(
        body,
        mesh=mesh,
        in_specs=(P("row", "col"),),
        out_specs=(P("row", "col"), P(None, ("row", "col"), None), P(None, ("row", "col"), None)),
        check_vma=False,
    )
```
